512 devices in a mesh: row: 32 (over x_lo, z), col: 16 (over y, x_hi, core).
Axes of the slice: x: 4 (x_hi: 2, x_lo: 2; x = x_hi * 2 + x_lo), y: 4, z: 16, core: 2. Of those that a mesh axis runs over, the one named last changes fastest.
Arguments:
- matrix: float32 [16384, 16384], P('row', 'col'), may hold values from -10 to 10, as said below
- vectors: float32 [2, 16384, 128], P(None, ('row', 'col')), may hold values from -0.09375 to 0.09375
- factors: float32 [2, 128, 128], replicated, may hold values from -0.5 to 1.5, as said below
Outputs:
- updated: float32 [16384, 16384], P('row', 'col')
The draws below stay inside these ranges and needn't reach their ends.
Inputs may be any that keep to these rules, and one draw needn't show every extreme that they name: matrix is exactly symmetric. Each factors[p] is upper triangular with a positive diagonal.
All inputs are finite; a program needn't handle non-finite values.
Results may differ from the reference program's by a relative error of at most 0.00013.
Values sent between devices are 32-bit elements; how exact they have to be, the bound alone decides.
No kernel may reach another device: no remote copies, remote signals or barrier semaphores. Data moves between devices by JAX's collectives and lax.ppermute only.
A program may use at most 64 MiB of HBM per device.

```python
import jax
import jax.numpy as jnp
from jax import lax

N = 16384
K = 128
PANELS = 2


def draw_matrix(key, part):
    key = jax.random.fold_in(key, 11)
    noise_key = jax.random.fold_in(key, 0)
    base = jnp.clip(jax.random.normal(noise_key, (N, N), jnp.float32), -5.0, 5.0)
    return (base + base.T) * 0.70710678


def draw_factors(key, part):
    key = jax.random.fold_in(key, 23)
    diag_key, off_key = jax.random.split(key)
    diag = jax.random.uniform(diag_key, (PANELS, K), jnp.float32, 0.5, 1.5)
    off = jnp.clip(jax.random.normal(off_key, (PANELS, K, K), jnp.float32), -4.0, 4.0) * (0.4 / K ** 0.5)
    rows = lax.broadcasted_iota(jnp.int32, (K, K), 0)
    cols = lax.broadcasted_iota(jnp.int32, (K, K), 1)
    upper = (cols > rows).astype(jnp.float32)
    eye = (cols == rows).astype(jnp.float32)
    return off * upper[None] + diag[:, :, None] * eye[None]


def steps_of(key, dims, pieces, smallest, top_value):
    factor_of = 1.0
    for position, blocks in pieces:
        draws = jax.random.uniform(jax.random.fold_in(jax.random.fold_in(key, 6), position), (blocks,), jnp.float32, smallest / len(pieces), top_value / len(pieces))
        factor_of = factor_of * jnp.repeat(jnp.exp(draws), dims[position] // blocks).reshape((-1,) + (1,) * (len(dims) - 1 - position))
    return factor_of


def scatter_about(key, extent, deviation, bound, cuts=(), dtype=jnp.bfloat16):
    result = deviation * jax.random.normal(key, extent, jnp.float32)
    if cuts:
        result = result * steps_of(key, extent, cuts, -0.22, 0.18)
    return jnp.clip(result, -bound, bound).astype(dtype)


def setup_inputs(seed: int = 0) -> dict:
    key_list = jax.random.split(jax.random.key(seed), 4)
    return {
        "matrix": draw_matrix(jax.random.fold_in(key_list[3], 71), 0),
        "vectors": scatter_about(key_list[1], (PANELS, N, K), (N // 4) ** -0.5, 0.09375, ((1, 512),), jnp.float32),
        "factors": draw_factors(jax.random.fold_in(key_list[3], 71), 0),
    }


HIGH = lax.Precision.HIGHEST


def reference(matrix, vectors, factors):
    current = matrix
    for panel in range(PANELS):
        basis = vectors[panel]
        factor = factors[panel]
        prod = jnp.dot(current, basis, precision=HIGH, preferred_element_type=jnp.float32)
        xmat = jnp.dot(prod, factor, precision=HIGH, preferred_element_type=jnp.float32)
        proj = lax.dot_general(basis, xmat, (((0,), (0,)), ((), ())), precision=HIGH, preferred_element_type=jnp.float32)
        inner = lax.dot_general(factor, proj, (((0,), (0,)), ((), ())), precision=HIGH, preferred_element_type=jnp.float32)
        wmat = xmat - 0.5 * jnp.dot(basis, inner, precision=HIGH, preferred_element_type=jnp.float32)
        first = lax.dot_general(basis, wmat, (((1,), (1,)), ((), ())), precision=HIGH, preferred_element_type=jnp.float32)
        second = lax.dot_general(wmat, basis, (((1,), (1,)), ((), ())), precision=HIGH, preferred_element_type=jnp.float32)
        current = current - first - second
    return current
```

```python
import jax
import jax.numpy as jnp
from jax import lax
from jax.sharding import Mesh, PartitionSpec as P

HIGH = lax.Precision.HIGH
HIGHEST = lax.Precision.HIGHEST
DEPTH = "z"
PLANE = ("y", "x_hi", "core", "x_lo")


def matmul(left, right, precision=HIGH):
    return jnp.dot(left, right, precision=precision, preferred_element_type=jnp.float32)


def contract_first(left, right, precision=HIGH):
    return lax.dot_general(
        left, right, (((0,), (0,)), ((), ())), precision=precision, preferred_element_type=jnp.float32
    )


def contract_last(left, right, precision=HIGH):
    return lax.dot_general(
        left, right, (((1,), (1,)), ((), ())), precision=precision, preferred_element_type=jnp.float32
    )


def exchange(parts, axes):
    return lax.all_to_all(parts, axes, 0, 0)


def spread(stack, own, extra=None):
    width = stack.shape[-1]
    cols = stack.reshape(8, 2, 2, 16, width).transpose(2, 0, 1, 3, 4).reshape(16, 1, 32, width)
    pieces = [jnp.broadcast_to(cols, (16, 2, 32, width)), jnp.broadcast_to(own[None], (16, 2, 16, width))]
    if extra is not None:
        pieces.append(jnp.broadcast_to(extra[None, None], (16, 2) + extra.shape))
    message = jnp.concatenate(pieces, axis=2)
    message = message.reshape((32,) + message.shape[2:])
    got = exchange(message, PLANE)
    col_rows = jnp.concatenate([got[:, :16].reshape(512, width), got[:, 16:32].reshape(512, width)], axis=0)
    row_rows = got[:, 32:48].reshape(512, width)
    if extra is None:
        return col_rows, row_rows
    return col_rows, row_rows, got[:, 48:].reshape(-1, width)


def coefficients(gram, factors):
    k = factors.shape[-1]
    f1, f2 = factors[0], factors[1]
    g11, g12, h12, g22 = gram[:k, :k], gram[:k, k:], gram[k:, :k], gram[k:, k:]
    mm = lambda a, b: matmul(a, b, HIGHEST)
    mt = lambda a, b: contract_first(a, b, HIGHEST)
    b1 = -0.5 * mt(f1, mm(g11, f1))
    m = mt(f1, g12) + mt(b1, h12)
    fh = mm(f1, h12)
    c = m + mm(b1, h12)
    s2 = mm(g22 - mt(g12, fh) - mt(h12, c), f2)
    b2 = -0.5 * mt(f2, s2)
    zero = jnp.zeros_like(f1)
    p = jnp.block([[f1, -mm(fh, f2)], [zero, f2]])
    q = jnp.block([[b1, -mm(c, f2)], [zero, b2]])
    return p, q


def body(matrix, vectors, factors):
    k = vectors.shape[-1]
    mine = jnp.concatenate([vectors[0], vectors[1]], axis=1)
    own_v = exchange(mine.reshape(2, 16, 2 * k), "x_lo")
    all_v = lax.all_gather(own_v, DEPTH)
    v_col, v_row = spread(all_v, own_v)
    part = matmul(matrix, v_col)
    gram = contract_first(v_row, part)
    flat = own_v.reshape(32, 2 * k)
    cross = contract_first(flat[:, :k], flat[:, k:])
    gram = jnp.concatenate([gram[:k], jnp.concatenate([cross, gram[k:, k:]], axis=1)], axis=0)
    sums = exchange(
        jnp.concatenate([part.reshape(32, 16, 2 * k), gram.reshape(32, 8, 2 * k)], axis=1), PLANE
    ).reshape(16, 2, 24, 2 * k)
    sums = jnp.sum(sums, axis=0)
    own_z = sums[:, :16]
    own_g = jnp.sum(sums[:, 16:], axis=0)
    gathered = lax.all_gather(jnp.concatenate([own_z.reshape(32, 2 * k), own_g], axis=0), DEPTH)
    all_z = gathered[:, :32].reshape(16, 2, 16, 2 * k)
    piece = jnp.sum(gathered[:, 32:], axis=0)
    z_col, z_row, gram = spread(all_z, own_z, piece)
    p, q = coefficients(gram, factors)
    left = jnp.concatenate([contract_last(v_row, p), matmul(z_row, p) + matmul(v_row, q + q.T)], axis=1)
    right = jnp.concatenate([z_col, v_col], axis=1)
    return matrix - contract_last(left, right)


def solution(mesh):
    fine = Mesh(mesh.devices.reshape(2, 16, 4, 2, 2), ("x_lo", "z", "y", "x_hi", "core"))
    row, col = ("x_lo", "z"), ("y", "x_hi", "core")
    in_specs = (P(row, col), P(None, row + col, None), P())
    return jax.shard_map(body, mesh=fine, in_specs=in_specs, out_specs=P(row, col), check_vma=False)
```

```python
import functools

import jax
import jax.numpy as jnp
from jax import lax
from jax.experimental import pallas as pl
from jax.experimental.pallas import tpu as pltpu
from jax.sharding import Mesh, PartitionSpec as P

DEPTH = "z"
PLANE = ("y", "x_hi", "core", "x_lo")
LIMIT = 48 * 1024 * 1024
CHUNKS = 4


def split(value):
    high = value.astype(jnp.bfloat16)
    return high, (value - high.astype(jnp.float32)).astype(jnp.bfloat16)


def product(left, right, dims):
    dot = functools.partial(
        lax.dot_general, dimension_numbers=(dims, ((), ())), preferred_element_type=jnp.float32
    )
    return dot(left[0], right[0]) + (dot(left[0], right[1]) + dot(left[1], right[0]))


def mm(left, right):
    return product(split(left), split(right), ((1,), (0,)))


def tm(left, right):
    return mm(left.T, right)


def mt(left, right):
    return product(split(left), split(right), ((1,), (1,)))


def part_kernel(matrix, got, own, message):
    k = own.shape[-1] // 2
    v0 = got[:, 0:16].reshape(512, 2 * k)
    v1 = got[:, 16:32].reshape(512, 2 * k)
    vr = got[:, 32:48].reshape(512, 2 * k)
    part = mm(matrix[:, :512], v0) + mm(matrix[:, 512:], v1)
    message[:, 0:16] = part.reshape(32, 16, 2 * k)
    gram = tm(vr, part)
    cross = tm(own[:, :k], own[:, k:])
    low = jnp.concatenate([cross, gram[k:, k:]], axis=1)
    message[0:16, 16:24] = gram[:k].reshape(16, 8, 2 * k)
    message[16:32, 16:24] = low.reshape(16, 8, 2 * k)


def update_kernel(matrix, got_v, got_z, factors, out, held, sems):
    k = factors.shape[-1]
    f1, f2 = factors[0], factors[1]
    gram = got_z[:, 48:56].reshape(2 * k, 2 * k)
    g11, g12, h12, g22 = gram[:k, :k], gram[:k, k:], gram[k:, :k], gram[k:, k:]
    b1 = -0.5 * tm(f1, mm(g11, f1))
    fh = mm(f1, h12)
    bh = mm(b1, h12)
    m = tm(f1, g12) + tm(b1, h12)
    c = m + bh
    s2 = mm(g22 - tm(g12, fh) - tm(h12, c), f2)
    b2 = -0.5 * tm(f2, s2)
    p12 = -mm(fh, f2)
    q12 = -mm(c, f2)
    zero = jnp.zeros_like(f1)
    p = split(jnp.concatenate([jnp.concatenate([f1, p12], axis=1), jnp.concatenate([zero, f2], axis=1)], axis=0))
    both = split(
        jnp.concatenate(
            [jnp.concatenate([b1 + b1.T, q12], axis=1), jnp.concatenate([q12.T, b2 + b2.T], axis=1)], axis=0
        )
    )
    v0 = split(got_v[:, 0:16].reshape(512, 2 * k))
    v1 = split(got_v[:, 16:32].reshape(512, 2 * k))
    z0 = split(got_z[:, 0:16].reshape(512, 2 * k))
    z1 = split(got_z[:, 16:32].reshape(512, 2 * k))
    last, inner = ((1,), (1,)), ((1,), (0,))
    rows = 512 // CHUNKS
    parts = 32 // CHUNKS
    copies = []
    for i in range(CHUNKS):
        here = slice(i * rows, (i + 1) * rows)
        vr = split(got_v[i * parts : (i + 1) * parts, 32:48].reshape(rows, 2 * k))
        zr = split(got_z[i * parts : (i + 1) * parts, 32:48].reshape(rows, 2 * k))
        on_z = split(product(vr, p, last))
        on_v = split(product(zr, p, inner) + product(vr, both, inner))
        held[here, :512] = matrix[here, :512] - product(on_z, z0, last) - product(on_v, v0, last)
        held[here, 512:] = matrix[here, 512:] - product(on_z, z1, last) - product(on_v, v1, last)
        copy = pltpu.make_async_copy(held.at[pl.ds(i * rows, rows)], out.at[pl.ds(i * rows, rows)], sems.at[i])
        copy.start()
        copies.append(copy)
    for copy in copies:
        copy.wait()


def part_of(matrix, got, own, interpret=False):
    return pl.pallas_call(
        part_kernel,
        out_shape=jax.ShapeDtypeStruct((32, 24, own.shape[-1]), jnp.float32),
        in_specs=[pl.BlockSpec(memory_space=pltpu.VMEM)] * 3,
        out_specs=pl.BlockSpec(memory_space=pltpu.VMEM),
        compiler_params=pltpu.CompilerParams(vmem_limit_bytes=LIMIT),
        interpret=interpret,
    )(matrix, got, own)


def updated_of(matrix, got_v, got_z, factors, interpret=False):
    return pl.pallas_call(
        update_kernel,
        out_shape=jax.ShapeDtypeStruct(matrix.shape, jnp.float32),
        in_specs=[pl.BlockSpec(memory_space=pltpu.VMEM)] * 4,
        out_specs=pl.BlockSpec(memory_space=pl.ANY),
        scratch_shapes=[pltpu.VMEM(matrix.shape, jnp.float32), pltpu.SemaphoreType.DMA((CHUNKS,))],
        compiler_params=pltpu.CompilerParams(vmem_limit_bytes=LIMIT),
        interpret=interpret,
    )(matrix, got_v, got_z, factors)


def exchange(parts, axes):
    return lax.all_to_all(parts, axes, 0, 0)


def spread(stack, own, extra=None):
    width = stack.shape[-1]
    cols = stack.reshape(8, 2, 2, 16, width).transpose(2, 0, 1, 3, 4).reshape(16, 1, 32, width)
    pieces = [jnp.broadcast_to(cols, (16, 2, 32, width)), jnp.broadcast_to(own[None], (16, 2, 16, width))]
    if extra is not None:
        pieces.append(jnp.broadcast_to(extra[None, None], (16, 2) + extra.shape))
    message = jnp.concatenate(pieces, axis=2)
    return exchange(message.reshape((32,) + message.shape[2:]), PLANE)


def body(matrix, vectors, factors):
    k = vectors.shape[-1]
    mine = jnp.concatenate([vectors[0], vectors[1]], axis=1)
    own_v = exchange(mine.reshape(2, 16, 2 * k), "x_lo")
    got_v = spread(lax.all_gather(own_v, DEPTH), own_v)
    sums = exchange(part_of(matrix, got_v, own_v.reshape(32, 2 * k)), PLANE)
    sums = jnp.sum(sums.reshape(16, 2, 24, 2 * k), axis=0)
    own_z = sums[:, :16]
    own_g = jnp.sum(sums[:, 16:], axis=0)
    gathered = lax.all_gather(jnp.concatenate([own_z.reshape(32, 2 * k), own_g], axis=0), DEPTH)
    got_z = spread(gathered[:, :32].reshape(16, 2, 16, 2 * k), own_z, jnp.sum(gathered[:, 32:], axis=0))
    return updated_of(matrix, got_v, got_z, factors)


def solution(mesh):
    fine = Mesh(mesh.devices.reshape(2, 16, 4, 2, 2), ("x_lo", "z", "y", "x_hi", "core"))
    row, col = ("x_lo", "z"), ("y", "x_hi", "core")
    in_specs = (P(row, col), P(None, row + col, None), P())
    return jax.shard_map(body, mesh=fine, in_specs=in_specs, out_specs=P(row, col), check_vma=False)
```

```python
import jax
import jax.numpy as jnp
from jax import lax
from jax.experimental import pallas as pl
from jax.experimental.pallas import tpu as pltpu
from jax.sharding import Mesh, PartitionSpec as P

COL = ("y", "x_hi", "core")
PLANE = COL + ("x_lo",)
RINGS = [[2 * z + (z + first) % 2 for z in range(16)] for first in range(2)]
LIMIT = 48 * 1024 * 1024
CHUNKS = 4
LAST, INNER = 1, 0


def split(value):
    high = value.astype(jnp.bfloat16)
    return high, (value - high.astype(jnp.float32)).astype(jnp.bfloat16)


def product(left, right, along):
    left, right = [split(a) for a in left], [split(b) for b in right]
    wide = [a[0] for a in left] + [a[1] for a in left] + [a[0] for a in left]
    tall = [b[0] for b in right] + [b[0] for b in right] + [b[1] for b in right]
    return lax.dot_general(
        jnp.concatenate(wide, axis=1),
        jnp.concatenate(tall, axis=along),
        (((1,), (along,)), ((), ())),
        preferred_element_type=jnp.float32,
    )


def mm(left, right):
    return product([left], [right], INNER)


def in_order(got, first, size, swap):
    parts = []
    for chip in range(8):
        for core in range(2):
            at = 4 * chip + 2 * (swap if core == 0 else 1 - swap)
            parts.append(got[pl.ds(at, 2), first : first + size].reshape(2 * size, got.shape[-1]))
    return jnp.concatenate(parts, axis=0)


def part_kernel(odd, matrix, got, own, message):
    k = own.shape[-1] // 2
    v0 = in_order(got, 0, 16, odd[0])
    v1 = in_order(got, 16, 16, 1 - odd[0])
    part = product([matrix[:, :512], matrix[:, 512:]], [v0, v1], INNER)
    message[:, 0:16] = part.reshape(32, 16, 2 * k)
    row = got[:, 32:48].reshape(512, 2 * k)
    gram = mm(row.T, part)
    cross = mm(own[:, :k].T, own[:, k:])
    low = jnp.concatenate([cross, gram[k:, k:]], axis=1)
    pieces = jnp.concatenate([gram[:k], low], axis=0).reshape(16, 2, 8, 2 * k)
    for chip in range(8):
        message[pl.ds(4 * chip + 2 * odd[0], 2), 16:24] = pieces[2 * chip]
        message[pl.ds(4 * chip + 2 * (1 - odd[0]), 2), 16:24] = pieces[2 * chip + 1]


def update_kernel(odd, matrix, got_v, got_z, factors, out, held, sems):
    k = factors.shape[-1]
    f1, f2 = factors[0], factors[1]
    gram = in_order(got_z, 48, 8, odd[0])
    g11, g12, h12, g22 = gram[:k, :k], gram[:k, k:], gram[k:, :k], gram[k:, k:]
    p12 = -mm(mm(f1, h12), f2)
    p = jnp.concatenate(
        [jnp.concatenate([f1, p12], axis=1), jnp.concatenate([jnp.zeros_like(f1), f2], axis=1)], axis=0
    )
    full = jnp.concatenate([gram[:k], jnp.concatenate([g12.T, g22], axis=1)], axis=0)
    gp = mm(full, p)
    v0 = in_order(got_v, 0, 16, odd[0])
    v1 = in_order(got_v, 16, 16, 1 - odd[0])
    z0 = in_order(got_z, 0, 16, odd[0])
    z1 = in_order(got_z, 16, 16, 1 - odd[0])
    rows = 512 // CHUNKS
    parts = 32 // CHUNKS
    copies = []
    for i in range(CHUNKS):
        here = slice(i * rows, (i + 1) * rows)
        vr = got_v[i * parts : (i + 1) * parts, 32:48].reshape(rows, 2 * k)
        zr = got_z[i * parts : (i + 1) * parts, 32:48].reshape(rows, 2 * k)
        on_z = product([vr], [p], LAST)
        on_v = product([zr, on_z], [p, -gp], INNER)
        held[here, :512] = matrix[here, :512] - product([on_z, on_v], [z0, v0], LAST)
        held[here, 512:] = matrix[here, 512:] - product([on_z, on_v], [z1, v1], LAST)
        copy = pltpu.make_async_copy(held.at[pl.ds(i * rows, rows)], out.at[pl.ds(i * rows, rows)], sems.at[i])
        copy.start()
        copies.append(copy)
    for copy in copies:
        copy.wait()


def part_of(*args):
    return pl.pallas_call(
        part_kernel,
        out_shape=jax.ShapeDtypeStruct((32, 24, args[-1].shape[-1]), jnp.float32),
        in_specs=[pl.BlockSpec(memory_space=pltpu.SMEM)] + [pl.BlockSpec(memory_space=pltpu.VMEM)] * 3,
        out_specs=pl.BlockSpec(memory_space=pltpu.VMEM),
        compiler_params=pltpu.CompilerParams(vmem_limit_bytes=LIMIT),
    )(*args)


def updated_of(*args):
    shape = args[1].shape
    return pl.pallas_call(
        update_kernel,
        out_shape=jax.ShapeDtypeStruct(shape, jnp.float32),
        in_specs=[pl.BlockSpec(memory_space=pltpu.SMEM)] + [pl.BlockSpec(memory_space=pltpu.VMEM)] * 4,
        out_specs=pl.BlockSpec(memory_space=pl.ANY),
        scratch_shapes=[pltpu.VMEM(shape, jnp.float32), pltpu.SemaphoreType.DMA((CHUNKS,))],
        compiler_params=pltpu.CompilerParams(vmem_limit_bytes=LIMIT),
    )(*args)


def exchange(parts, axes):
    return lax.all_to_all(parts, axes, 0, 0)


def gather(piece):
    return lax.all_gather(piece, ("z", "core"), axis_index_groups=RINGS)


def spread(stack, *common):
    width = stack.shape[-1]
    cols = stack.reshape(8, 2, 2, 16, width).transpose(2, 0, 1, 3, 4).reshape(16, 1, 32, width)
    pieces = [jnp.broadcast_to(cols, (16, 2, 32, width))]
    pieces += [jnp.broadcast_to(c[None], (16, 2) + c.shape[1:]) for c in common]
    message = jnp.concatenate(pieces, axis=2)
    return exchange(message.reshape((32,) + message.shape[2:]), PLANE)


def body(matrix, vectors, factors):
    k = vectors.shape[-1]
    mine = jnp.concatenate([vectors[0], vectors[1]], axis=1)
    odd = (lax.axis_index("z") % 2).reshape(1)
    half = lax.axis_index("x_lo")
    halves = mine.reshape(2, 16, 2 * k)
    theirs = lax.ppermute(jnp.where(half == 0, halves[1], halves[0]), "x_lo", [(0, 1), (1, 0)])
    own_v = jnp.stack([jnp.where(half == 0, halves[0], theirs), jnp.where(half == 0, theirs, halves[1])])
    got_v = spread(gather(own_v), own_v)
    sums = exchange(part_of(odd, matrix, got_v, own_v.reshape(32, 2 * k)), PLANE)
    sums = jnp.sum(sums.reshape(16, 2, 24, 2 * k), axis=0)
    own_z = sums[:, :16]
    own_g = jnp.sum(sums[:, 16:], axis=0)
    gathered = gather(jnp.concatenate([own_z.reshape(32, 2 * k), own_g], axis=0))
    got_z = spread(gathered[:, :32].reshape(16, 2, 16, 2 * k), own_z, jnp.sum(gathered[:, 32:], axis=0)[None])
    return updated_of(odd, matrix, got_v, got_z, factors)


def solution(mesh):
    fine = Mesh(mesh.devices.reshape(2, 16, 4, 2, 2), ("x_lo", "z", "y", "x_hi", "core"))
    row = ("x_lo", "z")
    in_specs = (P(row, COL), P(None, row + COL, None), P())
    return jax.shard_map(body, mesh=fine, in_specs=in_specs, out_specs=P(row, COL), check_vma=False)
```

```python
import jax
import jax.numpy as jnp
from jax import lax
from jax.experimental import pallas as pl
from jax.experimental.pallas import tpu as pltpu
from jax.sharding import Mesh, PartitionSpec as P

COL = ("y", "x_hi", "core")
PLANE = COL + ("x_lo",)
RINGS = [[2 * z + (z + first) % 2 for z in range(16)] for first in range(2)]
LIMIT = 48 * 1024 * 1024
CHUNKS = 4
LAST, INNER = 1, 0


def split(value):
    high = value.astype(jnp.bfloat16)
    return high, (value - high.astype(jnp.float32)).astype(jnp.bfloat16)


def product(left, right, along):
    return contract(thrice(left), right, along)


def thrice(left):
    left = [split(a) for a in left]
    return jnp.concatenate([a[0] for a in left] + [a[1] for a in left] + [a[0] for a in left], axis=1)


def contract(wide, right, along):
    right = [split(b) for b in right]
    tall = [b[0] for b in right] + [b[0] for b in right] + [b[1] for b in right]
    return lax.dot_general(
        wide,
        jnp.concatenate(tall, axis=along),
        (((1,), (along,)), ((), ())),
        preferred_element_type=jnp.float32,
    )


def mm(left, right):
    return product([left], [right], INNER)


def in_order(got, first, size, swap, chip_from=0, chips=8):
    parts = []
    for chip in range(chip_from, chip_from + chips):
        for core in range(2):
            at = 4 * chip + 2 * (swap if core == 0 else 1 - swap)
            parts.append(got[pl.ds(at, 2), first : first + size].reshape(2 * size, got.shape[-1]))
    return jnp.concatenate(parts, axis=0)


def part_kernel(odd, matrix, got, own, message):
    k = own.shape[-1] // 2
    v0 = in_order(got, 0, 16, odd[0])
    v1 = in_order(got, 16, 16, 1 - odd[0])
    part = product([matrix[:, :512], matrix[:, 512:]], [v0, v1], INNER)
    message[:, 0:16] = part.reshape(32, 16, 2 * k)
    row = got[:, 32:48].reshape(512, 2 * k)
    gram = mm(row.T, part)
    cross = mm(own[:, :k].T, own[:, k:])
    low = jnp.concatenate([cross, gram[k:, k:]], axis=1)
    pieces = jnp.concatenate([gram[:k], low], axis=0).reshape(16, 2, 8, 2 * k)
    for chip in range(8):
        message[pl.ds(4 * chip + 2 * odd[0], 2), 16:24] = pieces[2 * chip]
        message[pl.ds(4 * chip + 2 * (1 - odd[0]), 2), 16:24] = pieces[2 * chip + 1]


def update_kernel(odd, matrix, got_v, got_z, factors, out, held, sems):
    k = factors.shape[-1]
    f1, f2 = factors[0], factors[1]
    gram = in_order(got_z, 48, 8, odd[0])
    g11, g12, h12, g22 = gram[:k, :k], gram[:k, k:], gram[k:, :k], gram[k:, k:]
    p12 = -mm(mm(f1, h12), f2)
    p = jnp.concatenate(
        [jnp.concatenate([f1, p12], axis=1), jnp.concatenate([jnp.zeros_like(f1), f2], axis=1)], axis=0
    )
    full = jnp.concatenate([gram[:k], jnp.concatenate([g12.T, g22], axis=1)], axis=0)
    gp = mm(full, p)
    on_z = product([got_v[:, 32:48].reshape(512, 2 * k)], [p], LAST)
    on_v = product([got_z[:, 32:48].reshape(512, 2 * k), on_z], [p, -gp], INNER)
    left = thrice([on_z, on_v])
    chips = 16 // CHUNKS
    wide = 64 * chips
    copies = []
    for i in range(CHUNKS):
        half = 2 * i // CHUNKS
        swap = odd[0] if half == 0 else 1 - odd[0]
        first = i * chips - 8 * half
        z_col = in_order(got_z, 16 * half, 16, swap, first, chips)
        v_col = in_order(got_v, 16 * half, 16, swap, first, chips)
        here = slice(i * wide, (i + 1) * wide)
        held[:, here] = matrix[:, here] - contract(left, [z_col, v_col], LAST)
        there = pl.ds(i * wide, wide)
        copy = pltpu.make_async_copy(held.at[:, there], out.at[:, there], sems.at[i])
        copy.start()
        copies.append(copy)
    for copy in copies:
        copy.wait()


def part_of(*args):
    return pl.pallas_call(
        part_kernel,
        out_shape=jax.ShapeDtypeStruct((32, 24, args[-1].shape[-1]), jnp.float32),
        in_specs=[pl.BlockSpec(memory_space=pltpu.SMEM)] + [pl.BlockSpec(memory_space=pltpu.VMEM)] * 3,
        out_specs=pl.BlockSpec(memory_space=pltpu.VMEM),
        compiler_params=pltpu.CompilerParams(vmem_limit_bytes=LIMIT),
    )(*args)


def updated_of(*args):
    shape = args[1].shape
    return pl.pallas_call(
        update_kernel,
        out_shape=jax.ShapeDtypeStruct(shape, jnp.float32),
        in_specs=[pl.BlockSpec(memory_space=pltpu.SMEM)] + [pl.BlockSpec(memory_space=pltpu.VMEM)] * 4,
        out_specs=pl.BlockSpec(memory_space=pl.ANY),
        scratch_shapes=[pltpu.VMEM(shape, jnp.float32), pltpu.SemaphoreType.DMA((CHUNKS,))],
        compiler_params=pltpu.CompilerParams(vmem_limit_bytes=LIMIT),
    )(*args)


def exchange(parts, axes):
    return lax.all_to_all(parts, axes, 0, 0)


def gather(piece):
    return lax.all_gather(piece, ("z", "core"), axis_index_groups=RINGS)


def spread(stack, *common):
    width = stack.shape[-1]
    cols = stack.reshape(8, 2, 2, 16, width).transpose(2, 0, 1, 3, 4).reshape(16, 1, 32, width)
    pieces = [jnp.broadcast_to(cols, (16, 2, 32, width))]
    pieces += [jnp.broadcast_to(c[None], (16, 2) + c.shape[1:]) for c in common]
    message = jnp.concatenate(pieces, axis=2)
    return exchange(message.reshape((32,) + message.shape[2:]), PLANE)


def body(matrix, vectors, factors):
    k = vectors.shape[-1]
    mine = jnp.concatenate([vectors[0], vectors[1]], axis=1)
    odd = (lax.axis_index("z") & 1).reshape(1)
    half = lax.axis_index("x_lo")
    halves = mine.reshape(2, 16, 2 * k)
    theirs = lax.ppermute(jnp.where(half == 0, halves[1], halves[0]), "x_lo", [(0, 1), (1, 0)])
    own_v = jnp.stack([jnp.where(half == 0, halves[0], theirs), jnp.where(half == 0, theirs, halves[1])])
    odd, own_v = lax.optimization_barrier((odd, own_v))
    got_v = spread(gather(own_v), own_v)
    sums = exchange(part_of(odd, matrix, got_v, own_v.reshape(32, 2 * k)), PLANE)
    sums = jnp.sum(sums.reshape(16, 2, 24, 2 * k), axis=0)
    own_z = sums[:, :16]
    own_g = jnp.sum(sums[:, 16:], axis=0)
    gathered = gather(jnp.concatenate([own_z.reshape(32, 2 * k), own_g], axis=0))
    got_z = spread(gathered[:, :32].reshape(16, 2, 16, 2 * k), own_z, jnp.sum(gathered[:, 32:], axis=0)[None])
    return updated_of(odd, matrix, got_v, got_z, factors)


def solution(mesh):
    fine = Mesh(mesh.devices.reshape(2, 16, 4, 2, 2), ("x_lo", "z", "y", "x_hi", "core"))
    row = ("x_lo", "z")
    in_specs = (P(row, COL), P(None, row + COL, None), P())
    return jax.shard_map(body, mesh=fine, in_specs=in_specs, out_specs=P(row, COL), check_vma=False)
```

```python
import jax
import jax.numpy as jnp
from jax import lax
from jax.experimental import pallas as pl
from jax.experimental.pallas import tpu as pltpu
from jax.sharding import Mesh, PartitionSpec as P

COL = ("y", "x_hi", "core")
PLANE = COL + ("x_lo",)
RINGS = [[2 * z + (z + first) % 2 for z in range(16)] for first in range(2)]
LIMIT = 48 * 1024 * 1024
CHUNKS = 4
LAST, INNER = 1, 0


def split(value):
    high = value.astype(jnp.bfloat16)
    return high, (value - high.astype(jnp.float32)).astype(jnp.bfloat16)


def product(left, right, along):
    return contract(thrice(left), right, along)


def thrice(left):
    left = [split(a) for a in left]
    return jnp.concatenate([a[0] for a in left] + [a[1] for a in left] + [a[0] for a in left], axis=1)


def contract(wide, right, along):
    right = [split(b) for b in right]
    tall = [b[0] for b in right] + [b[0] for b in right] + [b[1] for b in right]
    return lax.dot_general(
        wide,
        jnp.concatenate(tall, axis=along),
        (((1,), (along,)), ((), ())),
        preferred_element_type=jnp.float32,
    )


def mm(left, right):
    return product([left], [right], INNER)


def in_order(got, first, size, swap, chip_from=0, chips=8):
    parts = []
    for chip in range(chip_from, chip_from + chips):
        for core in range(2):
            at = 4 * chip + 2 * (swap if core == 0 else 1 - swap)
            parts.append(got[pl.ds(at, 2), first : first + size].reshape(2 * size, got.shape[-1]))
    return jnp.concatenate(parts, axis=0)


def part_kernel(odd, core, matrix, got, own, message):
    k = own.shape[-1] // 2
    v0 = in_order(got, 0, 16, odd[0])
    v1 = in_order(got, 16, 16, 1 - odd[0])
    part = product([matrix[:, :512], matrix[:, 512:]], [v0, v1], INNER)
    slots = (core[0], 1 - core[0])
    for chip in range(8):
        for other in range(2):
            piece = part[64 * chip + 32 * other : 64 * chip + 32 * other + 32].reshape(1, 2, 16, 2 * k)
            message[pl.ds(slots[other], 1), 2 * chip : 2 * chip + 2, 0:16] = piece
    row = got[:, 32:48].reshape(512, 2 * k)
    gram = mm(row.T, part)
    cross = mm(own[:, :k].T, own[:, k:])
    low = jnp.concatenate([cross, gram[k:, k:]], axis=1)
    pieces = jnp.concatenate([gram[:k], low], axis=0).reshape(16, 2, 8, 2 * k)
    flips = (odd[0] ^ core[0], 1 - (odd[0] ^ core[0]))
    for chip in range(8):
        for ring in range(2):
            piece = pieces[2 * chip + ring].reshape(1, 2, 8, 2 * k)
            message[pl.ds(flips[ring], 1), 2 * chip : 2 * chip + 2, 16:24] = piece


def update_kernel(odd, matrix, got_v, got_z, factors, out, held, sems):
    k = factors.shape[-1]
    f1, f2 = factors[0], factors[1]
    gram = in_order(got_z, 48, 8, odd[0])
    g11, g12, h12, g22 = gram[:k, :k], gram[:k, k:], gram[k:, :k], gram[k:, k:]
    p12 = -mm(mm(f1, h12), f2)
    p = jnp.concatenate(
        [jnp.concatenate([f1, p12], axis=1), jnp.concatenate([jnp.zeros_like(f1), f2], axis=1)], axis=0
    )
    full = jnp.concatenate([gram[:k], jnp.concatenate([g12.T, g22], axis=1)], axis=0)
    gp = mm(full, p)
    on_z = product([got_v[:, 32:48].reshape(512, 2 * k)], [p], LAST)
    on_v = product([got_z[:, 32:48].reshape(512, 2 * k), on_z], [p, -gp], INNER)
    left = thrice([on_z, on_v])
    chips = 16 // CHUNKS
    wide = 64 * chips
    copies = []
    for i in range(CHUNKS):
        half = 2 * i // CHUNKS
        swap = odd[0] if half == 0 else 1 - odd[0]
        first = i * chips - 8 * half
        z_col = in_order(got_z, 16 * half, 16, swap, first, chips)
        v_col = in_order(got_v, 16 * half, 16, swap, first, chips)
        here = slice(i * wide, (i + 1) * wide)
        held[:, here] = matrix[:, here] - contract(left, [z_col, v_col], LAST)
        there = pl.ds(i * wide, wide)
        copy = pltpu.make_async_copy(held.at[:, there], out.at[:, there], sems.at[i])
        copy.start()
        copies.append(copy)
    for copy in copies:
        copy.wait()


def part_of(*args):
    return pl.pallas_call(
        part_kernel,
        out_shape=jax.ShapeDtypeStruct((2, 16, 24, args[-1].shape[-1]), jnp.float32),
        in_specs=[pl.BlockSpec(memory_space=pltpu.SMEM)] * 2 + [pl.BlockSpec(memory_space=pltpu.VMEM)] * 3,
        out_specs=pl.BlockSpec(memory_space=pltpu.VMEM),
        compiler_params=pltpu.CompilerParams(vmem_limit_bytes=LIMIT),
    )(*args)


def updated_of(*args):
    shape = args[1].shape
    return pl.pallas_call(
        update_kernel,
        out_shape=jax.ShapeDtypeStruct(shape, jnp.float32),
        in_specs=[pl.BlockSpec(memory_space=pltpu.SMEM)] + [pl.BlockSpec(memory_space=pltpu.VMEM)] * 4,
        out_specs=pl.BlockSpec(memory_space=pl.ANY),
        scratch_shapes=[pltpu.VMEM(shape, jnp.float32), pltpu.SemaphoreType.DMA((CHUNKS,))],
        compiler_params=pltpu.CompilerParams(vmem_limit_bytes=LIMIT),
    )(*args)


def exchange(parts, axes):
    return lax.all_to_all(parts, axes, 0, 0)


def gather(piece):
    return lax.all_gather(piece, ("z", "core"), axis_index_groups=RINGS)


def spread(stack, *common):
    width = stack.shape[-1]
    cols = stack.reshape(8, 2, 2, 16, width).transpose(2, 0, 1, 3, 4).reshape(16, 1, 32, width)
    pieces = [jnp.broadcast_to(cols, (16, 2, 32, width))]
    pieces += [jnp.broadcast_to(c[None], (16, 2) + c.shape[1:]) for c in common]
    message = jnp.concatenate(pieces, axis=2)
    return exchange(message.reshape((32,) + message.shape[2:]), PLANE)


def body(matrix, vectors, factors):
    k = vectors.shape[-1]
    mine = jnp.concatenate([vectors[0], vectors[1]], axis=1)
    odd = (lax.axis_index("z") & 1).reshape(1)
    half = lax.axis_index("x_lo")
    halves = mine.reshape(2, 16, 2 * k)
    theirs = lax.ppermute(jnp.where(half == 0, halves[1], halves[0]), "x_lo", [(0, 1), (1, 0)])
    own_v = jnp.stack([jnp.where(half == 0, halves[0], theirs), jnp.where(half == 0, theirs, halves[1])])
    core = lax.axis_index("core").reshape(1)
    near = lax.axis_index("core") == 0
    odd, core, near, own_v = lax.optimization_barrier((odd, core, near, own_v))
    got_v = spread(gather(own_v), own_v)
    message = part_of(odd, core, matrix, got_v, own_v.reshape(32, 2 * k))
    both = lax.all_gather(message[1], "core")
    pair = message[0] + jnp.where(near, both[1], both[0])
    sums = jnp.sum(exchange(pair, ("y", "x_hi", "x_lo")).reshape(8, 2, 24, 2 * k), axis=0)
    own_z = sums[:, :16]
    own_g = jnp.sum(sums[:, 16:], axis=0)
    gathered = gather(jnp.concatenate([own_z.reshape(32, 2 * k), own_g], axis=0))
    got_z = spread(gathered[:, :32].reshape(16, 2, 16, 2 * k), own_z, jnp.sum(gathered[:, 32:], axis=0)[None])
    return updated_of(odd, matrix, got_v, got_z, factors)


def solution(mesh):
    fine = Mesh(mesh.devices.reshape(2, 16, 4, 2, 2), ("x_lo", "z", "y", "x_hi", "core"))
    row = ("x_lo", "z")
    in_specs = (P(row, COL), P(None, row + COL, None), P())
    return jax.shard_map(body, mesh=fine, in_specs=in_specs, out_specs=P(row, COL), check_vma=False)
```

```python
import jax
import jax.numpy as jnp
from jax import lax
from jax.experimental import pallas as pl
from jax.experimental.pallas import tpu as pltpu
from jax.sharding import Mesh, PartitionSpec as P

COL = ("y", "x_hi", "core")
PLANE = COL + ("x_lo",)
RINGS = [[2 * z + (z + first) % 2 for z in range(16)] for first in range(2)]
LIMIT = 48 * 1024 * 1024
CHUNKS = 4
LAST, INNER = 1, 0


def split(value):
    high = value.astype(jnp.bfloat16)
    return high, (value - high.astype(jnp.float32)).astype(jnp.bfloat16)


def product(left, right, along):
    return contract(thrice(left), right, along)


def thrice(left):
    left = [split(a) for a in left]
    return jnp.concatenate([a[0] for a in left] + [a[1] for a in left] + [a[0] for a in left], axis=1)


def contract(wide, right, along):
    right = [split(b) for b in right]
    tall = [b[0] for b in right] + [b[0] for b in right] + [b[1] for b in right]
    return lax.dot_general(
        wide,
        jnp.concatenate(tall, axis=along),
        (((1,), (along,)), ((), ())),
        preferred_element_type=jnp.float32,
    )


def mm(left, right):
    return product([left], [right], INNER)


def in_order(got, first, size, swap, chip_from=0, chips=8):
    parts = []
    for chip in range(chip_from, chip_from + chips):
        for core in range(2):
            at = 4 * chip + 2 * (swap if core == 0 else 1 - swap)
            parts.append(got[pl.ds(at, 2), first : first + size].reshape(2 * size, got.shape[-1]))
    return jnp.concatenate(parts, axis=0)


def part_kernel(odd, core, matrix, got, own, message):
    k = own.shape[-1] // 2
    v0 = in_order(got, 0, 16, odd[0])
    v1 = in_order(got, 16, 16, 1 - odd[0])
    part = product([matrix[:, :512], matrix[:, 512:]], [v0, v1], INNER)
    slots = (core[0], 1 - core[0])
    for chip in range(8):
        for other in range(2):
            piece = part[64 * chip + 32 * other : 64 * chip + 32 * other + 32].reshape(1, 2, 16, 2 * k)
            message[pl.ds(slots[other], 1), 2 * chip : 2 * chip + 2, 0:16] = piece
    row = got[:, 32:48].reshape(512, 2 * k)
    gram = mm(row.T, part)
    cross = mm(own[:, :k].T, own[:, k:])
    low = jnp.concatenate([cross, gram[k:, k:]], axis=1)
    pieces = jnp.concatenate([gram[:k], low], axis=0).reshape(16, 2, 8, 2 * k)
    flips = (odd[0] ^ core[0], 1 - (odd[0] ^ core[0]))
    for chip in range(8):
        for ring in range(2):
            piece = pieces[2 * chip + ring].reshape(1, 2, 8, 2 * k)
            message[pl.ds(flips[ring], 1), 2 * chip : 2 * chip + 2, 16:24] = piece


def update_kernel(odd, matrix, got_v, got_z, factors, out, held, sems):
    k = factors.shape[-1]
    f1, f2 = factors[0], factors[1]
    gram = in_order(got_z, 48, 8, odd[0])
    g11, g12, h12, g22 = gram[:k, :k], gram[:k, k:], gram[k:, :k], gram[k:, k:]
    p12 = -mm(mm(f1, h12), f2)
    p = jnp.concatenate(
        [jnp.concatenate([f1, p12], axis=1), jnp.concatenate([jnp.zeros_like(f1), f2], axis=1)], axis=0
    )
    full = jnp.concatenate([gram[:k], jnp.concatenate([g12.T, g22], axis=1)], axis=0)
    gp = mm(full, p)
    on_z = product([got_v[:, 32:48].reshape(512, 2 * k)], [p], LAST)
    on_v = product([got_z[:, 32:48].reshape(512, 2 * k), on_z], [p, -gp], INNER)
    left = thrice([on_z, on_v])
    chips = 16 // CHUNKS
    wide = 64 * chips
    copies = []
    for i in range(CHUNKS):
        half = 2 * i // CHUNKS
        swap = odd[0] if half == 0 else 1 - odd[0]
        first = i * chips - 8 * half
        z_col = in_order(got_z, 16 * half, 16, swap, first, chips)
        v_col = in_order(got_v, 16 * half, 16, swap, first, chips)
        here = slice(i * wide, (i + 1) * wide)
        held[:, here] = matrix[:, here] - contract(left, [z_col, v_col], LAST)
        there = pl.ds(i * wide, wide)
        copy = pltpu.make_async_copy(held.at[:, there], out.at[:, there], sems.at[i])
        copy.start()
        copies.append(copy)
    for copy in copies:
        copy.wait()


def part_of(*args):
    return pl.pallas_call(
        part_kernel,
        out_shape=jax.ShapeDtypeStruct((2, 16, 24, args[-1].shape[-1]), jnp.float32),
        in_specs=[pl.BlockSpec(memory_space=pltpu.SMEM)] * 2 + [pl.BlockSpec(memory_space=pltpu.VMEM)] * 3,
        out_specs=pl.BlockSpec(memory_space=pltpu.VMEM),
        compiler_params=pltpu.CompilerParams(vmem_limit_bytes=LIMIT),
    )(*args)


def updated_of(*args):
    shape = args[1].shape
    return pl.pallas_call(
        update_kernel,
        out_shape=jax.ShapeDtypeStruct(shape, jnp.float32),
        in_specs=[pl.BlockSpec(memory_space=pltpu.SMEM)] + [pl.BlockSpec(memory_space=pltpu.VMEM)] * 4,
        out_specs=pl.BlockSpec(memory_space=pl.ANY),
        scratch_shapes=[pltpu.VMEM(shape, jnp.float32), pltpu.SemaphoreType.DMA((CHUNKS,))],
        compiler_params=pltpu.CompilerParams(vmem_limit_bytes=LIMIT),
    )(*args)


def exchange(parts, axes):
    return lax.all_to_all(parts, axes, 0, 0)


def gather(piece):
    return lax.all_gather(piece, ("z", "core"), axis_index_groups=RINGS)


def spread(stack, *common):
    width = stack.shape[-1]
    cols = stack.reshape(8, 2, 2, 16, width).transpose(2, 0, 1, 3, 4).reshape(16, 1, 32, width)
    pieces = [jnp.broadcast_to(cols, (16, 2, 32, width))]
    pieces += [jnp.broadcast_to(c[None], (16, 2) + c.shape[1:]) for c in common]
    message = jnp.concatenate(pieces, axis=2)
    return exchange(message.reshape((32,) + message.shape[2:]), PLANE)


def body(matrix, vectors, factors):
    k = vectors.shape[-1]
    odd = (lax.axis_index("z") & 1).reshape(1)
    left = lax.axis_index("x_lo") == 0
    pair = lax.all_gather(vectors, "x_lo")
    half = jnp.where(left, pair[:, :, :16], pair[:, :, 16:])
    own_v = jnp.concatenate([half[:, 0], half[:, 1]], axis=-1)
    core = lax.axis_index("core").reshape(1)
    near = lax.axis_index("core") == 0
    odd, core, near, own_v = lax.optimization_barrier((odd, core, near, own_v))
    got_v = spread(gather(own_v), own_v)
    message = part_of(odd, core, matrix, got_v, own_v.reshape(32, 2 * k))
    both = lax.all_gather(message[1], "core")
    pair = message[0] + jnp.where(near, both[1], both[0])
    sums = jnp.sum(exchange(pair, ("y", "x_hi", "x_lo")).reshape(8, 2, 24, 2 * k), axis=0)
    own_z = sums[:, :16]
    own_g = jnp.sum(sums[:, 16:], axis=0)
    gathered = gather(jnp.concatenate([own_z.reshape(32, 2 * k), own_g], axis=0))
    got_z = spread(gathered[:, :32].reshape(16, 2, 16, 2 * k), own_z, jnp.sum(gathered[:, 32:], axis=0)[None])
    return updated_of(odd, matrix, got_v, got_z, factors)


def solution(mesh):
    fine = Mesh(mesh.devices.reshape(2, 16, 4, 2, 2), ("x_lo", "z", "y", "x_hi", "core"))
    row = ("x_lo", "z")
    in_specs = (P(row, COL), P(None, row + COL, None), P())
    return jax.shard_map(body, mesh=fine, in_specs=in_specs, out_specs=P(row, COL), check_vma=False)
```

```python
import jax
import jax.numpy as jnp
from jax import lax
from jax.experimental import pallas as pl
from jax.experimental.pallas import tpu as pltpu
from jax.sharding import Mesh, PartitionSpec as P

COL = ("y", "x_hi", "core")
PLANE = COL + ("x_lo",)
RINGS = [[2 * z + (z + first) % 2 for z in range(16)] for first in range(2)]
LIMIT = 48 * 1024 * 1024
CHUNKS = 4
LAST, INNER = 1, 0


def split(value):
    high = value.astype(jnp.bfloat16)
    return high, (value - high.astype(jnp.float32)).astype(jnp.bfloat16)


def product(left, right, along):
    return contract(thrice(left), right, along)


def thrice(left):
    left = [split(a) for a in left]
    return jnp.concatenate([a[0] for a in left] + [a[1] for a in left] + [a[0] for a in left], axis=1)


def contract(wide, right, along):
    right = [split(b) for b in right]
    tall = [b[0] for b in right] + [b[0] for b in right] + [b[1] for b in right]
    return lax.dot_general(
        wide,
        jnp.concatenate(tall, axis=along),
        (((1,), (along,)), ((), ())),
        preferred_element_type=jnp.float32,
    )


def mm(left, right):
    return product([left], [right], INNER)


def in_order(got, first, size, swap, chip_from=0, chips=8):
    parts = []
    for chip in range(chip_from, chip_from + chips):
        for core in range(2):
            at = 4 * chip + 2 * (swap if core == 0 else 1 - swap)
            parts.append(got[pl.ds(at, 2), first : first + size].reshape(2 * size, got.shape[-1]))
    return jnp.concatenate(parts, axis=0)


def part_kernel(odd, core, matrix, got, own, message):
    k = own.shape[-1] // 2
    v0 = in_order(got, 0, 16, odd[0])
    v1 = in_order(got, 16, 16, 1 - odd[0])
    part = product([matrix[:, :512], matrix[:, 512:]], [v0, v1], INNER)
    slots = (core[0], 1 - core[0])
    for chip in range(8):
        for other in range(2):
            piece = part[64 * chip + 32 * other : 64 * chip + 32 * other + 32].reshape(1, 2, 16, 2 * k)
            message[pl.ds(slots[other], 1), 2 * chip : 2 * chip + 2, 0:16] = piece
    row = got[:, 32:48].reshape(512, 2 * k)
    gram = mm(row.T, part)
    cross = mm(own[:, :k].T, own[:, k:])
    low = jnp.concatenate([cross, gram[k:, k:]], axis=1)
    pieces = jnp.concatenate([gram[:k], low], axis=0).reshape(16, 2, 8, 2 * k)
    flips = (odd[0] ^ core[0], 1 - (odd[0] ^ core[0]))
    for chip in range(8):
        for ring in range(2):
            piece = pieces[2 * chip + ring].reshape(1, 2, 8, 2 * k)
            message[pl.ds(flips[ring], 1), 2 * chip : 2 * chip + 2, 16:24] = piece


def update_kernel(odd, matrix, got_v, got_z, halves, factors, out, held, sems):
    k = factors.shape[-1]
    f1, f2 = factors[0], factors[1]
    gram = in_order(got_z, 40, 8, odd[0])
    g11, g12, h12, g22 = gram[:k, :k], gram[:k, k:], gram[k:, :k], gram[k:, k:]
    p12 = -mm(mm(f1, h12), f2)
    p = jnp.concatenate(
        [jnp.concatenate([f1, p12], axis=1), jnp.concatenate([jnp.zeros_like(f1), f2], axis=1)], axis=0
    )
    full = jnp.concatenate([gram[:k], jnp.concatenate([g12.T, g22], axis=1)], axis=0)
    gp = mm(full, p)
    on_z = product([got_v[:, 32:48].reshape(512, 2 * k)], [p], LAST)
    z_row = jnp.concatenate([halves[0], halves[1]], axis=1).reshape(512, 2 * k)
    on_v = product([z_row, on_z], [p, -gp], INNER)
    left = thrice([on_z, on_v])
    chips = 16 // CHUNKS
    wide = 64 * chips
    copies = []
    for i in range(CHUNKS):
        half = 2 * i // CHUNKS
        swap = odd[0] if half == 0 else 1 - odd[0]
        first = i * chips - 8 * half
        z_col = in_order(got_z, 16 * half, 16, swap, first, chips)
        v_col = in_order(got_v, 16 * half, 16, swap, first, chips)
        here = slice(i * wide, (i + 1) * wide)
        held[:, here] = matrix[:, here] - contract(left, [z_col, v_col], LAST)
        there = pl.ds(i * wide, wide)
        copy = pltpu.make_async_copy(held.at[:, there], out.at[:, there], sems.at[i])
        copy.start()
        copies.append(copy)
    for copy in copies:
        copy.wait()


def part_of(*args):
    return pl.pallas_call(
        part_kernel,
        out_shape=jax.ShapeDtypeStruct((2, 16, 24, args[-1].shape[-1]), jnp.float32),
        in_specs=[pl.BlockSpec(memory_space=pltpu.SMEM)] * 2 + [pl.BlockSpec(memory_space=pltpu.VMEM)] * 3,
        out_specs=pl.BlockSpec(memory_space=pltpu.VMEM),
        compiler_params=pltpu.CompilerParams(vmem_limit_bytes=LIMIT),
    )(*args)


def updated_of(*args):
    shape = args[1].shape
    return pl.pallas_call(
        update_kernel,
        out_shape=jax.ShapeDtypeStruct(shape, jnp.float32),
        in_specs=[pl.BlockSpec(memory_space=pltpu.SMEM)] + [pl.BlockSpec(memory_space=pltpu.VMEM)] * 5,
        out_specs=pl.BlockSpec(memory_space=pl.ANY),
        scratch_shapes=[pltpu.VMEM(shape, jnp.float32), pltpu.SemaphoreType.DMA((CHUNKS,))],
        compiler_params=pltpu.CompilerParams(vmem_limit_bytes=LIMIT),
    )(*args)


def exchange(parts, axes):
    return lax.all_to_all(parts, axes, 0, 0)


def gather(piece):
    return lax.all_gather(piece, ("z", "core"), axis_index_groups=RINGS)


def spread(stack, *common):
    width = stack.shape[-1]
    cols = stack.reshape(8, 2, 2, 16, width).transpose(2, 0, 1, 3, 4).reshape(16, 1, 32, width)
    pieces = [jnp.broadcast_to(cols, (16, 2, 32, width))]
    pieces += [jnp.broadcast_to(c, (8, 2, 2) + c.shape[2:]).reshape((16, 2) + c.shape[2:]) for c in common]
    message = jnp.concatenate(pieces, axis=2)
    return exchange(message.reshape((32,) + message.shape[2:]), PLANE)


def body(matrix, vectors, factors):
    k = vectors.shape[-1]
    odd = (lax.axis_index("z") & 1).reshape(1)
    left = lax.axis_index("x_lo") == 0
    pair = lax.all_gather(vectors, "x_lo")
    half = jnp.where(left, pair[:, :, :16], pair[:, :, 16:])
    own_v = jnp.concatenate([half[:, 0], half[:, 1]], axis=-1)
    core = lax.axis_index("core").reshape(1)
    near = lax.axis_index("core") == 0
    odd, core, near, own_v = lax.optimization_barrier((odd, core, near, own_v))
    got_v = spread(gather(own_v), own_v[None])
    message = part_of(odd, core, matrix, got_v, own_v.reshape(32, 2 * k))
    both = lax.all_gather(message[1], "core")
    pair = message[0] + jnp.where(near, both[1], both[0])
    sums = jnp.sum(exchange(pair, ("y", "x_hi", "x_lo")).reshape(8, 2, 24, 2 * k), axis=0)
    own_z = sums[:, :16]
    own_g = jnp.sum(sums[:, 16:], axis=0)
    gathered = gather(jnp.concatenate([own_z.reshape(32, 2 * k), own_g], axis=0))
    split_z = own_z.reshape(2, 2, 8, 2 * k).transpose(1, 0, 2, 3)
    total_g = jnp.sum(gathered[:, 32:], axis=0)[None, None]
    got_z = spread(gathered[:, :32].reshape(16, 2, 16, 2 * k), split_z, total_g)
    halves = lax.all_gather(got_z[:, 32:40], "core")
    return updated_of(odd, matrix, got_v, got_z, halves, factors)


def solution(mesh):
    fine = Mesh(mesh.devices.reshape(2, 16, 4, 2, 2), ("x_lo", "z", "y", "x_hi", "core"))
    row = ("x_lo", "z")
    in_specs = (P(row, COL), P(None, row + COL, None), P())
    return jax.shard_map(body, mesh=fine, in_specs=in_specs, out_specs=P(row, COL), check_vma=False)
```

```python
import jax
import jax.numpy as jnp
from jax import lax
from jax.experimental import pallas as pl
from jax.experimental.pallas import tpu as pltpu
from jax.sharding import Mesh, PartitionSpec as P

COL = ("y", "x_hi", "core")
PLANE = COL + ("x_lo",)
RINGS = [[2 * z + (z + first) % 2 for z in range(16)] for first in range(2)]
LIMIT = 48 * 1024 * 1024
CHUNKS = 4
LAST, INNER = 1, 0


def split(value):
    high = value.astype(jnp.bfloat16)
    return high, (value - high.astype(jnp.float32)).astype(jnp.bfloat16)


def product(left, right, along):
    return contract(thrice(left), right, along)


def thrice(left):
    left = [split(a) for a in left]
    return jnp.concatenate([a[0] for a in left] + [a[1] for a in left] + [a[0] for a in left], axis=1)


def contract(wide, right, along):
    right = [split(b) for b in right]
    tall = [b[0] for b in right] + [b[0] for b in right] + [b[1] for b in right]
    return lax.dot_general(
        wide,
        jnp.concatenate(tall, axis=along),
        (((1,), (along,)), ((), ())),
        preferred_element_type=jnp.float32,
    )


def mm(left, right):
    return product([left], [right], INNER)


def over_rows(left, right):
    left, right = split(left), split(right)
    return lax.dot_general(
        jnp.concatenate([left[0], left[1], left[0]], axis=0),
        jnp.concatenate([right[0], right[0], right[1]], axis=0),
        (((0,), (0,)), ((), ())),
        preferred_element_type=jnp.float32,
    )


def in_order(got, first, size, swap, chip_from=0, chips=8):
    parts = []
    for chip in range(chip_from, chip_from + chips):
        for core in range(2):
            at = 4 * chip + 2 * (swap if core == 0 else 1 - swap)
            parts.append(got[pl.ds(at, 2), first : first + size].reshape(2 * size, got.shape[-1]))
    return jnp.concatenate(parts, axis=0)


def part_kernel(odd, core, matrix, got, own, message):
    k = own.shape[-1] // 2
    v0 = in_order(got, 0, 16, odd[0])
    v1 = in_order(got, 16, 16, 1 - odd[0])
    part = product([matrix[:, :512], matrix[:, 512:]], [v0, v1], INNER)
    slots = (core[0], 1 - core[0])
    for chip in range(8):
        for other in range(2):
            piece = part[64 * chip + 32 * other : 64 * chip + 32 * other + 32].reshape(1, 2, 16, 2 * k)
            message[pl.ds(slots[other], 1), 2 * chip : 2 * chip + 2, 0:16] = piece
    row = got[:, 32:48].reshape(512, 2 * k)
    gram = over_rows(row, part)
    cross = over_rows(own[:, :k], own[:, k:])
    low = jnp.concatenate([cross, gram[k:, k:]], axis=1)
    pieces = jnp.concatenate([gram[:k], low], axis=0).reshape(16, 2, 8, 2 * k)
    flips = (odd[0] ^ core[0], 1 - (odd[0] ^ core[0]))
    for chip in range(8):
        for ring in range(2):
            piece = pieces[2 * chip + ring].reshape(1, 2, 8, 2 * k)
            message[pl.ds(flips[ring], 1), 2 * chip : 2 * chip + 2, 16:24] = piece


def update_kernel(odd, matrix, got_v, got_z, factors, out, held, sems):
    k = factors.shape[-1]
    f1, f2 = factors[0], factors[1]
    gram = in_order(got_z, 48, 8, odd[0])
    g11, g12, h12, g22 = gram[:k, :k], gram[:k, k:], gram[k:, :k], gram[k:, k:]
    p12 = -mm(mm(f1, h12), f2)
    p = jnp.concatenate(
        [jnp.concatenate([f1, p12], axis=1), jnp.concatenate([jnp.zeros_like(f1), f2], axis=1)], axis=0
    )
    full = jnp.concatenate([gram[:k], jnp.concatenate([g12.T, g22], axis=1)], axis=0)
    gp = mm(full, p)
    on_z = product([got_v[:, 32:48].reshape(512, 2 * k)], [p], LAST)
    on_v = product([got_z[:, 32:48].reshape(512, 2 * k), on_z], [p, -gp], INNER)
    left = thrice([on_z, on_v])
    chips = 16 // CHUNKS
    wide = 64 * chips
    copies = []
    for i in range(CHUNKS):
        half = 2 * i // CHUNKS
        swap = odd[0] if half == 0 else 1 - odd[0]
        first = i * chips - 8 * half
        z_col = in_order(got_z, 16 * half, 16, swap, first, chips)
        v_col = in_order(got_v, 16 * half, 16, swap, first, chips)
        here = slice(i * wide, (i + 1) * wide)
        held[:, here] = matrix[:, here] - contract(left, [z_col, v_col], LAST)
        there = pl.ds(i * wide, wide)
        copy = pltpu.make_async_copy(held.at[:, there], out.at[:, there], sems.at[i])
        copy.start()
        copies.append(copy)
    for copy in copies:
        copy.wait()


def part_of(*args):
    return pl.pallas_call(
        part_kernel,
        out_shape=jax.ShapeDtypeStruct((2, 16, 24, args[-1].shape[-1]), jnp.float32),
        in_specs=[pl.BlockSpec(memory_space=pltpu.SMEM)] * 2 + [pl.BlockSpec(memory_space=pltpu.VMEM)] * 3,
        out_specs=pl.BlockSpec(memory_space=pltpu.VMEM),
        compiler_params=pltpu.CompilerParams(vmem_limit_bytes=LIMIT),
    )(*args)


def updated_of(*args):
    shape = args[1].shape
    return pl.pallas_call(
        update_kernel,
        out_shape=jax.ShapeDtypeStruct(shape, jnp.float32),
        in_specs=[pl.BlockSpec(memory_space=pltpu.SMEM)] + [pl.BlockSpec(memory_space=pltpu.VMEM)] * 4,
        out_specs=pl.BlockSpec(memory_space=pl.ANY),
        scratch_shapes=[pltpu.VMEM(shape, jnp.float32), pltpu.SemaphoreType.DMA((CHUNKS,))],
        compiler_params=pltpu.CompilerParams(vmem_limit_bytes=LIMIT),
    )(*args)


def exchange(parts, axes):
    return lax.all_to_all(parts, axes, 0, 0)


def gather(piece):
    return lax.all_gather(piece, ("z", "core"), axis_index_groups=RINGS)


def spread(stack, *common):
    width = stack.shape[-1]
    cols = stack.reshape(8, 2, 2, 16, width).transpose(2, 0, 1, 3, 4).reshape(16, 1, 32, width)
    pieces = [jnp.broadcast_to(cols, (16, 2, 32, width))]
    pieces += [jnp.broadcast_to(c[None], (16, 2) + c.shape[1:]) for c in common]
    message = jnp.concatenate(pieces, axis=2)
    return exchange(message.reshape((32,) + message.shape[2:]), PLANE)


def body(matrix, vectors, factors):
    k = vectors.shape[-1]
    odd = (lax.axis_index("z") & 1).reshape(1)
    left = lax.axis_index("x_lo") == 0
    pair = lax.all_gather(vectors, "x_lo")
    half = jnp.where(left, pair[:, :, :16], pair[:, :, 16:])
    own_v = jnp.concatenate([half[:, 0], half[:, 1]], axis=-1)
    core = lax.axis_index("core").reshape(1)
    near = lax.axis_index("core") == 0
    odd, core, near, own_v = lax.optimization_barrier((odd, core, near, own_v))
    got_v = spread(gather(own_v), own_v)
    message = part_of(odd, core, matrix, got_v, own_v.reshape(32, 2 * k))
    both = lax.all_gather(message[1], "core")
    pair = message[0] + jnp.where(near, both[1], both[0])
    sums = jnp.sum(exchange(pair, ("y", "x_hi", "x_lo")).reshape(8, 2, 24, 2 * k), axis=0)
    own_z = sums[:, :16]
    own_g = jnp.sum(sums[:, 16:], axis=0)
    gathered = gather(jnp.concatenate([own_z.reshape(32, 2 * k), own_g], axis=0))
    got_z = spread(gathered[:, :32].reshape(16, 2, 16, 2 * k), own_z, jnp.sum(gathered[:, 32:], axis=0)[None])
    return updated_of(odd, matrix, got_v, got_z, factors)


def solution(mesh):
    fine = Mesh(mesh.devices.reshape(2, 16, 4, 2, 2), ("x_lo", "z", "y", "x_hi", "core"))
    row = ("x_lo", "z")
    in_specs = (P(row, COL), P(None, row + COL, None), P())
    return jax.shard_map(body, mesh=fine, in_specs=in_specs, out_specs=P(row, COL), check_vma=False)
```
